32 devices in a mesh: groups: 2 (over y), hid: 4 (over x, core), mdl: 4 (over z).
Axes of the slice: x: 2, y: 2, z: 4, core: 2. Of those that a mesh axis runs over, the one named last changes fastest.
Arguments:
- tokens: bfloat16 [32, 2, 8192], P('groups', None, 'mdl'), parts along dimension 0, may hold values from -6 to 6
- norm_gain: bfloat16 [8192], P('mdl'), may hold values from 0.25 to 1.75
- query_weight: bfloat16 [8192, 8192], P('mdl', 'hid'), may hold values from -0.0625 to 0.0625
- key_weight: bfloat16 [8192, 1024], P('mdl', 'hid'), may hold values from -0.0625 to 0.0625
- value_weight: bfloat16 [8192, 1024], P('mdl', 'hid'), may hold values from -0.0625 to 0.0625
- query_bias: bfloat16 [8192], P('hid'), may hold values from -3 to 3
- key_bias: bfloat16 [1024], P('hid'), may hold values from -3 to 3
- value_bias: bfloat16 [1024], P('hid'), may hold values from -3 to 3
- out_weight: bfloat16 [8192, 8192], P('hid', 'mdl'), may hold values from -4 to 4
- key_cache: bfloat16 [32, 4096, 1024], P(('groups', 'hid'), 'mdl'), parts along dimension 0, may hold values from -500 to 500
- value_cache: bfloat16 [32, 4096, 1024], P(('groups', 'hid'), 'mdl'), parts along dimension 0, may hold values from -6 to 6
- lengths: int32 [32], P('groups'), parts along dimension 0, may hold values from 512 to 4096, as said below
Outputs:
- attention_out: bfloat16 [32, 2, 8192], P(('groups', 'hid'), None, 'mdl'), parts along dimension 0
The draws below stay inside these ranges and needn't reach their ends.
There are 2 independent parts, one for each index of `groups`. The reference program is written for one: setup_inputs(seed, part) draws one part's arguments, and reference() takes and returns one part's arrays. A program takes and returns all parts, laid end to end along the dimension named above; an argument that names none is the same for every part. Nothing has to cross between parts.
Inputs may be any that keep to these rules, and one draw needn't show every extreme that they name: `lengths`: one row of each part holds 4096 keys and another 4096 / 8.
All inputs are finite; a program needn't handle non-finite values.
Results may differ from the reference program's by a relative error of at most 0.03.
Values may be sent and summed in bfloat16 or wider, within the bound.
A program may use at most 128 MiB of HBM per device.

```python
import math
import jax
import jax.numpy as jnp
from jax import lax

D = 8192
HEADS = 64
KV_HEADS = 8
HEAD_DIM = 128
CACHE = 4096
STEPS = 2
ROWS = 16


def draw_key_cache(key, part):
    key = jax.random.fold_in(key, 11)
    key_base = jax.random.fold_in(key, 0)
    width = KV_HEADS * HEAD_DIM
    result = jnp.clip(jax.random.normal(key_base, (ROWS, CACHE, width), jnp.float32), -6.0, 6.0)
    return result.astype(jnp.bfloat16)


def draw_lengths(key, part):
    key = jax.random.fold_in(key, 5)
    key_base, key_first, key_gap = jax.random.split(key, 3)
    lowest = CACHE // 8
    drawn = jax.random.randint(key_base, (ROWS,), lowest, CACHE + 1)
    first_row = jax.random.randint(key_first, (), 0, ROWS)
    row_gap = jax.random.randint(key_gap, (), 1, ROWS)
    other_row = (first_row + row_gap) % ROWS
    row_index = jnp.arange(ROWS, dtype=jnp.int32)
    drawn = jnp.where(row_index == first_row, CACHE, drawn)
    drawn = jnp.where(row_index == other_row, lowest, drawn)
    return drawn.astype(jnp.int32)


def block_levels(rng, shape, cuts, low, top_value):
    loudness = 1.0
    for axis_at, shards_of in cuts:
        steps = jax.random.uniform(jax.random.fold_in(jax.random.fold_in(rng, 6), axis_at), (shards_of,), jnp.float32, low / len(cuts), top_value / len(cuts))
        loudness = loudness * jnp.repeat(jnp.exp(steps), shape[axis_at] // shards_of).reshape((-1,) + (1,) * (len(shape) - 1 - axis_at))
    return loudness


def gaussian(stream_key, dims, scale, reach, pieces=(), kind=jnp.bfloat16):
    level = block_levels(stream_key, dims, pieces, -0.22, 0.18) if pieces else 1.0
    values = jax.random.normal(stream_key, dims, jnp.float32) * scale * level
    return jnp.minimum(jnp.maximum(values, -reach), reach).astype(kind)


def setup_inputs(seed: int = 0, part: int = 0) -> dict:
    splits = jax.random.split(jax.random.key(seed), 13)
    own_keys = jax.random.split(jax.random.fold_in(splits[12], part), 13)
    return {
        "tokens": gaussian(own_keys[0], (ROWS, STEPS, D), 1.0, 6.0, ((2, 4),)),
        "norm_gain": jnp.clip(1.0 + 0.15 * jax.random.normal(splits[1], (D,), jnp.float32), 0.25, 1.75).astype(jnp.bfloat16),
        "query_weight": gaussian(splits[2], (D, HEADS * HEAD_DIM), D ** -0.5, 0.0625, ((0, 4), (1, 4))),
        "key_weight": gaussian(splits[3], (D, KV_HEADS * HEAD_DIM), D ** -0.5, 0.0625, ((0, 4), (1, 4))),
        "value_weight": gaussian(splits[4], (D, KV_HEADS * HEAD_DIM), D ** -0.5, 0.0625, ((0, 4), (1, 4))),
        "query_bias": gaussian(splits[5], (HEADS * HEAD_DIM,), 0.5, 3.0, ((0, 4),)),
        "key_bias": gaussian(splits[6], (KV_HEADS * HEAD_DIM,), 0.5, 3.0, ((0, 4),)),
        "value_bias": gaussian(splits[7], (KV_HEADS * HEAD_DIM,), 0.5, 3.0, ((0, 4),)),
        "out_weight": gaussian(splits[8], (HEADS * HEAD_DIM, D), (HEADS * HEAD_DIM // CACHE) ** -0.5, 4.0, ((0, 4), (1, 4))),
        "key_cache": draw_key_cache(jax.random.fold_in(jax.random.fold_in(splits[12], part), 71), part),
        "value_cache": gaussian(own_keys[10], (ROWS, CACHE, KV_HEADS * HEAD_DIM), 1.0, 6.0, ((0, 4), (1, 4))),
        "lengths": draw_lengths(jax.random.fold_in(jax.random.fold_in(splits[12], part), 71), part),
    }


epsilon = 1e-06
rope_base = 1000000.0

def rotate_pairs(values, positions):
    half = values.shape[-1] // 2
    freq = rope_base ** (-jnp.arange(half, dtype=jnp.float32) * 2.0 / values.shape[-1])
    angles = positions.astype(jnp.float32)[..., None, None] * freq
    cosine = jnp.cos(angles)
    sine = jnp.sin(angles)
    lower = values[..., :half]
    upper = values[..., half:]
    return jnp.concatenate([lower * cosine - upper * sine, upper * cosine + lower * sine], axis=-1)

def attend_row(items):
    row_queries, row_keys, row_values, cache_keys, cache_values, length = items
    group = HEADS // KV_HEADS
    grouped = row_queries.reshape(STEPS, KV_HEADS, group, HEAD_DIM).transpose(1, 0, 2, 3)
    grouped = grouped.reshape(KV_HEADS, STEPS * group, HEAD_DIM).astype(jnp.float32)
    keys_all = cache_keys.reshape(CACHE, KV_HEADS, HEAD_DIM).astype(jnp.float32)
    values_all = cache_values.reshape(CACHE, KV_HEADS, HEAD_DIM).astype(jnp.float32)
    score_scale = 1.0 / math.sqrt(HEAD_DIM)
    scores = jnp.einsum('kqd,skd->kqs', grouped, keys_all) * score_scale
    visible = (jnp.arange(CACHE, dtype=jnp.int32) < length)[None, None, :]
    new_scores = jnp.einsum('kqd,ukd->kqu', grouped, row_keys.astype(jnp.float32)) * score_scale
    query_step = jnp.arange(STEPS * group, dtype=jnp.int32) // group
    causal = (jnp.arange(STEPS, dtype=jnp.int32)[None, :] <= query_step[:, None])[None]
    overall = jnp.maximum(lax.optimization_barrier(jnp.max(jnp.where(visible, scores, -jnp.inf), axis=-1)), lax.optimization_barrier(jnp.max(jnp.where(causal, new_scores, -jnp.inf), axis=-1)))
    cache_weights = jnp.exp(jnp.where(visible, scores - overall[..., None], -jnp.inf))
    new_weights = jnp.exp(jnp.where(causal, new_scores - overall[..., None], -jnp.inf))
    denom = lax.optimization_barrier(jnp.sum(cache_weights, axis=-1)) + lax.optimization_barrier(jnp.sum(new_weights, axis=-1))
    cache_rounded = lax.optimization_barrier(cache_weights.astype(jnp.bfloat16)).astype(jnp.float32)
    new_rounded = lax.optimization_barrier(new_weights.astype(jnp.bfloat16)).astype(jnp.float32)
    summed = jnp.einsum('kqs,skd->kqd', cache_rounded, values_all)
    summed = summed + jnp.einsum('kqu,ukd->kqd', new_rounded, row_values.astype(jnp.float32))
    result = summed / denom[..., None]
    result = result.reshape(KV_HEADS, STEPS, group, HEAD_DIM).transpose(1, 0, 2, 3)
    return result.reshape(STEPS, HEADS * HEAD_DIM).astype(jnp.bfloat16)

def reference(tokens, norm_gain, query_weight, key_weight, value_weight, query_bias, key_bias, value_bias, out_weight, key_cache, value_cache, lengths):
    inputs = tokens.astype(jnp.float32)
    inv_rms = lax.rsqrt(lax.optimization_barrier(jnp.mean(inputs * inputs, axis=-1)) + epsilon)
    scaled = (inputs * norm_gain.astype(jnp.float32)).astype(jnp.bfloat16).reshape(ROWS * STEPS, D)
    row_scale = inv_rms.reshape(ROWS * STEPS, 1)

    def project(weight, bias):
        product = jnp.dot(scaled, weight, preferred_element_type=jnp.float32)
        return (product * row_scale + bias.astype(jnp.float32)).astype(jnp.bfloat16)
    query_lin = project(query_weight, query_bias).reshape(ROWS, STEPS, HEADS, HEAD_DIM)
    key_lin = project(key_weight, key_bias).reshape(ROWS, STEPS, KV_HEADS, HEAD_DIM)
    value_new = project(value_weight, value_bias).reshape(ROWS, STEPS, KV_HEADS, HEAD_DIM)
    positions = lengths[:, None] + jnp.arange(STEPS, dtype=jnp.int32)[None, :]
    queries = rotate_pairs(query_lin.astype(jnp.float32), positions).astype(jnp.bfloat16)
    key_new = rotate_pairs(key_lin.astype(jnp.float32), positions).astype(jnp.bfloat16)
    attended = lax.map(attend_row, (queries, key_new, value_new, key_cache, value_cache, lengths))
    flat = attended.reshape(ROWS * STEPS, HEADS * HEAD_DIM)
    result = jnp.dot(flat, out_weight, preferred_element_type=jnp.float32)
    return result.astype(jnp.bfloat16).reshape(ROWS, STEPS, D)
```

```python
import math

import jax
import jax.numpy as jnp
import numpy as np
from jax import lax
from jax.experimental import pallas as pl
from jax.experimental.pallas import tpu as pltpu
from jax.sharding import PartitionSpec as P

D = 8192
HEADS = 64
KV_HEADS = 8
HEAD_DIM = 128


epsilon = 1e-06
rope_base = 1000000.0


def combined_all(value, axis, combine):
    everything = jax.tree.map(
        lambda part, kind: lax.all_gather(part.astype(kind), axis),
        value,
        (jnp.bfloat16, jnp.bfloat16, jnp.bfloat16),
    )

    def take(k):
        return jax.tree.map(lambda part, own: part[k].astype(own.dtype), everything, value)

    return lax.fori_loop(
        1, lax.axis_size(axis), lambda k, so_far: combine(so_far, take(k)), take(0)
    )


def rotate_pairs(values, positions):
    half = values.shape[-1] // 2
    freq = rope_base ** (-jnp.arange(half, dtype=jnp.float32) * 2.0 / values.shape[-1])
    angles = positions.astype(jnp.float32)[..., None, None] * freq
    cosine = jnp.cos(angles)
    sine = jnp.sin(angles)
    lower = values[..., :half]
    upper = values[..., half:]
    return jnp.concatenate([lower * cosine - upper * sine, upper * cosine + lower * sine], axis=-1)


def join_parts(left_part, right_part):
    left_max, left_sum, left_acc = left_part
    right_max, right_sum, right_acc = right_part
    joined_max = jnp.maximum(left_max, right_max)
    left_factor = jnp.exp(left_max - joined_max)
    right_factor = jnp.exp(right_max - joined_max)
    joined_sum = left_sum * left_factor + right_sum * right_factor
    joined_acc = left_acc * left_factor[..., None] + right_acc * right_factor[..., None]
    return (joined_max, joined_sum, joined_acc)


def body(
    tokens,
    norm_gain,
    query_weight,
    key_weight,
    value_weight,
    query_bias,
    key_bias,
    value_bias,
    out_weight,
    key_cache,
    value_cache,
    lengths,
):
    row_count = tokens.shape[0]
    steps_count = tokens.shape[1]
    hid_count = lax.axis_size("hid")
    local_rows = key_cache.shape[0]
    local_len = key_cache.shape[1]
    group = HEADS // KV_HEADS
    query_width = query_weight.shape[1]
    key_width = key_weight.shape[1]
    proj_width = query_width + 2 * key_width
    inputs = tokens.astype(jnp.float32)
    square_sum = lax.psum(jnp.sum(inputs * inputs, axis=-1), "mdl")
    inv_rms = lax.rsqrt(square_sum / D + epsilon)
    row_scale = inv_rms.reshape(row_count * steps_count, 1)
    scaled = (
        (inputs * norm_gain.astype(jnp.float32))
        .astype(jnp.bfloat16)
        .reshape(row_count * steps_count, -1)
    )
    partial_value = jnp.concatenate(
        [
            jnp.dot(scaled, query_weight, preferred_element_type=jnp.float32),
            jnp.dot(scaled, key_weight, preferred_element_type=jnp.float32),
            jnp.dot(scaled, value_weight, preferred_element_type=jnp.float32),
        ],
        axis=1,
    )
    all_bias = jnp.concatenate([query_bias, key_bias, value_bias]).astype(jnp.float32)
    summed = lax.psum(partial_value.astype(jnp.bfloat16), "mdl").astype(jnp.float32)
    projected = (
        (summed * row_scale + all_bias)
        .astype(jnp.bfloat16)
        .reshape(row_count, steps_count, proj_width)
    )
    arrived = lax.all_to_all(projected, "hid", split_axis=0, concat_axis=2, tiled=True)
    blocks = arrived.reshape(local_rows, steps_count, hid_count, proj_width)
    query_lin = blocks[..., :query_width].reshape(local_rows, steps_count, HEADS, HEAD_DIM)
    key_lin = blocks[..., query_width : query_width + key_width].reshape(
        local_rows, steps_count, KV_HEADS, HEAD_DIM
    )
    value_new = blocks[..., query_width + key_width :].reshape(
        local_rows, steps_count, KV_HEADS, HEAD_DIM
    )
    my_lengths = lax.dynamic_slice_in_dim(
        lengths, lax.axis_index("hid") * local_rows, local_rows, 0
    )
    positions = my_lengths[:, None] + jnp.arange(steps_count, dtype=jnp.int32)[None, :]
    queries = rotate_pairs(query_lin.astype(jnp.float32), positions).astype(jnp.bfloat16)
    key_new = rotate_pairs(key_lin.astype(jnp.float32), positions).astype(jnp.bfloat16)
    grouped = queries.reshape(local_rows, steps_count, KV_HEADS, group, HEAD_DIM).transpose(
        0, 2, 1, 3, 4
    )
    grouped = grouped.reshape(local_rows, KV_HEADS, steps_count * group, HEAD_DIM)
    cache_keys = key_cache.reshape(local_rows, local_len, KV_HEADS, HEAD_DIM)
    cache_values = value_cache.reshape(local_rows, local_len, KV_HEADS, HEAD_DIM)
    score_scale = 1.0 / math.sqrt(HEAD_DIM)
    scores = (
        jnp.einsum("rkqd,rskd->rkqs", grouped, cache_keys, preferred_element_type=jnp.float32)
        * score_scale
    )
    cache_place = lax.axis_index("mdl") * local_len + jnp.arange(local_len, dtype=jnp.int32)
    visible = (cache_place[None, :] < my_lengths[:, None])[:, None, None, :]
    masked = jnp.where(visible, scores, -1e30)
    local_max = jnp.max(masked, axis=-1)
    weights = jnp.where(visible, jnp.exp(masked - local_max[..., None]), 0.0)
    local_sum = jnp.sum(weights, axis=-1)
    local_acc = jnp.einsum(
        "rkqs,rskd->rkqd",
        weights.astype(jnp.bfloat16),
        cache_values,
        preferred_element_type=jnp.float32,
    )
    run_max, run_sum, run_acc = combined_all((local_max, local_sum, local_acc), "mdl", join_parts)
    new_scores = (
        jnp.einsum("rkqd,rukd->rkqu", grouped, key_new, preferred_element_type=jnp.float32)
        * score_scale
    )
    query_step = jnp.arange(steps_count * group, dtype=jnp.int32) // group
    causal = (jnp.arange(steps_count, dtype=jnp.int32)[None, :] <= query_step[:, None])[None, None]
    new_masked = jnp.where(causal, new_scores, -1e30)
    new_max = jnp.maximum(run_max, jnp.max(new_masked, axis=-1))
    shrink = jnp.exp(run_max - new_max)
    new_weights = jnp.where(causal, jnp.exp(new_masked - new_max[..., None]), 0.0)
    total = run_sum * shrink + jnp.sum(new_weights, axis=-1)
    combined = run_acc * shrink[..., None] + jnp.einsum(
        "rkqu,rukd->rkqd",
        new_weights.astype(jnp.bfloat16),
        value_new,
        preferred_element_type=jnp.float32,
    )
    attended = combined / total[..., None]
    attended = attended.reshape(local_rows, KV_HEADS, steps_count, group, HEAD_DIM).transpose(
        0, 2, 1, 3, 4
    )
    attended = attended.reshape(local_rows, steps_count, HEADS * HEAD_DIM).astype(jnp.bfloat16)
    by_heads = lax.all_to_all(attended, "hid", split_axis=2, concat_axis=0, tiled=True)
    flat_heads = by_heads.reshape(row_count * steps_count, query_width)
    result = lax.psum_scatter(
        jnp.dot(flat_heads, out_weight, preferred_element_type=jnp.float32).astype(jnp.bfloat16),
        "hid",
        scatter_dimension=0,
        tiled=True,
    )
    return result.reshape(local_rows, steps_count, -1)

def fused_kernel(
    tokens_ref, gain_ref, bias_ref, freq_ref, lengths_ref, query_hbm, key_hbm, value_hbm, out_hbm, keys_hbm, values_hbm,
    result_ref,
    proj_w, out_w, keys, values,
    send1, recv1, squares, recv_squares, send2, recv2, rotated, key_rot, value_rot, row_queries, row_keys, row_values,
    send3, recv3, stats, recv_stats, send4, recv4, heads_f32, heads_in, partial_out, send5, recv5,
    load_sem, s1, r1, sq_s, sq_r, s2, r2, s3, r3, st_s, st_r, s4, r4, s5, r5,
):
    hid_count, mdl_count = lax.axis_size("hid"), lax.axis_size("mdl")
    me_h, me_m = lax.axis_index("hid"), lax.axis_index("mdl")
    bf16, f32 = jnp.bfloat16, jnp.float32
    rows = tokens_ref.shape[0]
    own_rows = rows // hid_count
    local_rows, local_len = keys.shape[0], keys.shape[1]
    heads_out = proj_w.shape[2] // HEAD_DIM
    query_width, key_width = query_hbm.shape[1], key_hbm.shape[1]
    query_heads = query_width // HEAD_DIM
    kv_local = key_width // HEAD_DIM
    group = HEADS // KV_HEADS
    block_rows = 2 * group
    block_width = proj_w.shape[2]

    def send(src, dst, send_sem, recv_sem, to):
        return pltpu.make_async_remote_copy(
            src_ref=src, dst_ref=dst, send_sem=send_sem, recv_sem=recv_sem,
            device_id=to, device_id_type=pl.DeviceIdType.MESH,
        )

    loads = []

    def load(src, dst):
        copy = pltpu.make_async_copy(src, dst, load_sem.at[len(loads)])
        copy.start()
        loads.append(copy)
        return copy

    block_loads = []
    parts = ((query_hbm, 0, query_width), (key_hbm, query_width, key_width), (value_hbm, query_width + key_width, key_width))
    for b in range(mdl_count):
        low, high = b * block_width, (b + 1) * block_width
        mine = []
        for ref, base, width in parts:
            first, last = max(low, base), min(high, base + width)
            if first < last:
                mine.append(load(ref.at[:, first - base : last - base], proj_w.at[b, :, first - low : last - low]))
        block_loads.append(mine)
    keys_load = load(keys_hbm, keys)
    values_load = load(values_hbm, values)
    out_load = load(out_hbm, out_w)

    others = [(dh, dm) for dh in range(hid_count) for dm in range(mdl_count) if dh or dm]

    def partner(dh, dm):
        return {"hid": lax.rem(me_h + dh, hid_count), "mdl": lax.rem(me_m + dm, mdl_count)}

    barrier = pltpu.get_barrier_semaphore()
    for dh, dm in others:
        pl.semaphore_signal(barrier, inc=1, device_id=partner(dh, dm), device_id_type=pl.DeviceIdType.MESH)

    inputs = tokens_ref[...].astype(f32)
    square_col = jnp.sum(inputs * inputs, axis=-1, keepdims=True)
    eye_in = (
        lax.broadcasted_iota(jnp.int32, (rows, 128), 0) == lax.broadcasted_iota(jnp.int32, (rows, 128), 1)
    )
    square_row = jnp.sum(jnp.where(eye_in, square_col, 0.0), axis=0, keepdims=True)
    squares[...] = jnp.broadcast_to(square_row, squares.shape)
    scaled = (inputs * gain_ref[...].astype(f32)).astype(bf16)
    pl.semaphore_wait(barrier, len(others))

    square_copies = []
    for d in range(1, mdl_count):
        copy = send(squares, recv_squares.at[d], sq_s.at[d], sq_r.at[d], partner(0, d))
        copy.start()
        square_copies.append(copy)

    def block_copy(d):
        b = lax.rem(me_m + d, mdl_count)
        return send(send1.at[b], recv1.at[d], s1.at[d], r1.at[d], {"mdl": b})

    for b in range(mdl_count):
        for copy in block_loads[b]:
            copy.wait()
        part = jnp.dot(scaled, proj_w[b], preferred_element_type=f32).astype(bf16)
        for i in range(heads_out):
            send1[b, i] = part[:, i * HEAD_DIM : (i + 1) * HEAD_DIM]

        @pl.when(me_m != b)
        def _():
            block_copy(lax.rem(b - me_m + mdl_count, mdl_count)).start()

    place = lax.broadcasted_iota(jnp.int32, (own_rows, HEAD_DIM), 0)
    lane = lax.broadcasted_iota(jnp.int32, (own_rows, HEAD_DIM), 1)
    position = place % 2
    for r in range(local_rows):
        position = position + jnp.where(place // 2 == r, lengths_ref[me_h * local_rows + r], 0)
    half = HEAD_DIM // 2
    angles = position.astype(f32) * freq_ref[...]
    cosine = jnp.cos(angles)
    sine = jnp.sin(angles)
    sine = jnp.where(lane < half, -sine, sine)

    for copy in square_copies:
        copy.wait()
    square_total = squares[...]
    for d in range(1, mdl_count):
        square_total = square_total + recv_squares[d]
    square_sum = jnp.sum(jnp.where(eye_in, square_total[:1, :], 0.0), axis=1, keepdims=True)
    inv_rms = lax.rsqrt(square_sum / D + epsilon)
    for d in range(1, mdl_count):
        block_copy(d).wait()
    for i in range(heads_out):
        total = send1[me_m, i].astype(f32)
        for d in range(1, mdl_count):
            total = total + recv1[d, i].astype(f32)
        total = total * inv_rms + bias_ref[me_m, i]
        for h in range(hid_count):
            send2[h, i] = total[h * own_rows : (h + 1) * own_rows].astype(bf16)
    recv2[me_h, me_m] = send2[me_h]
    copies = []
    for k, (dh, dm) in enumerate(others):
        to = partner(dh, dm)
        copy = send(send2.at[to["hid"]], recv2.at[me_h, me_m], s2.at[k], r2.at[k], to)
        copy.start()
        copies.append(copy)
    for copy in copies:
        copy.wait()

    for h in range(hid_count):
        x = recv2[h].astype(f32).reshape(mdl_count * heads_out, own_rows, HEAD_DIM)
        turn = x[: query_heads + kv_local].reshape((query_heads + kv_local) * own_rows, HEAD_DIM)
        turned = turn.reshape(-1, own_rows, HEAD_DIM) * cosine[None] + pltpu.roll(turn, half, 1).reshape(
            -1, own_rows, HEAD_DIM
        ) * sine[None]
        n = query_heads * own_rows
        rotated[h * n : (h + 1) * n] = turned[:query_heads].reshape(n, HEAD_DIM)
        n = kv_local * own_rows
        key_rot[h * n : (h + 1) * n] = turned[query_heads:].astype(bf16).astype(f32).reshape(n, HEAD_DIM)
        value_rot[h * n : (h + 1) * n] = x[query_heads + kv_local :].reshape(n, HEAD_DIM)
    for r in range(local_rows):
        steps = [rotated[pl.ds(2 * r + t, HEADS, stride=own_rows), :] for t in range(2)]
        for kv in range(KV_HEADS):
            row_queries[r, kv] = jnp.concatenate(
                [s[kv * group : (kv + 1) * group] for s in steps], axis=0
            ).astype(bf16)
        for t in range(2):
            row_keys[r, t] = key_rot[pl.ds(2 * r + t, KV_HEADS, stride=own_rows), :]
            row_values[r, t] = value_rot[pl.ds(2 * r + t, KV_HEADS, stride=own_rows), :]

    keys_load.wait()
    values_load.wait()
    score_scale = 1.0 / math.sqrt(HEAD_DIM)
    pair_rows = 2 * block_rows
    columns = lax.broadcasted_iota(jnp.int32, (pair_rows, local_len), 1)
    all_rows = KV_HEADS * block_rows
    eye = (
        lax.broadcasted_iota(jnp.int32, (all_rows, 128), 0) == lax.broadcasted_iota(jnp.int32, (all_rows, 128), 1)
    )

    def to_row(col):
        return jnp.sum(jnp.where(eye, col, 0.0), axis=0, keepdims=True)

    def to_col(row):
        return jnp.sum(jnp.where(eye, row, 0.0), axis=1, keepdims=True)

    def part_copy(d):
        to = {"mdl": lax.rem(me_m + d, mdl_count)}
        return send(send3.at[d], recv3.at[d], s3.at[d], r3.at[d], to)

    def stat_copy(d):
        to = {"mdl": lax.rem(me_m + d, mdl_count)}
        return send(stats.at[d], recv_stats.at[d], st_s.at[d], st_r.at[d], to)

    def one_row(step, carry):
        d = lax.rem(step, mdl_count)
        r = lax.rem(me_m + d, mdl_count)
        visible = columns < lengths_ref[me_h * local_rows + r] - me_m * local_len
        tops, sums = [], []
        for p in range(KV_HEADS // 2):
            qa, qb = row_queries[r, 2 * p], row_queries[r, 2 * p + 1]
            none = jnp.zeros_like(qa)
            left = jnp.concatenate(
                [jnp.concatenate([qa, none], axis=1), jnp.concatenate([none, qb], axis=1)], axis=0
            )
            wide = slice(p * 2 * HEAD_DIM, (p + 1) * 2 * HEAD_DIM)
            scores = lax.dot_general(
                left, keys[r, :, wide], (((1,), (1,)), ((), ())), preferred_element_type=f32
            ) * score_scale
            masked = jnp.where(visible, scores, -1e30)
            top = jnp.max(masked, axis=-1, keepdims=True)
            weights = jnp.where(visible, jnp.exp(masked - top), 0.0)
            tops.append(top)
            sums.append(jnp.sum(weights, axis=-1, keepdims=True))
            acc = jnp.dot(weights.astype(bf16), values[r, :, wide], preferred_element_type=f32)
            send3[d, 2 * p] = acc[:block_rows, :HEAD_DIM].astype(bf16)
            send3[d, 2 * p + 1] = acc[block_rows:, HEAD_DIM:].astype(bf16)
        stats[d, 0] = jnp.broadcast_to(to_row(jnp.concatenate(tops, axis=0)), (8, 128))
        stats[d, 1] = jnp.broadcast_to(to_row(jnp.concatenate(sums, axis=0)), (8, 128))

        @pl.when(d != 0)
        def _():
            part_copy(d).start()
            stat_copy(d).start()

        return carry

    lax.fori_loop(1, mdl_count + 1, one_row, 0)

    query_all = row_queries[me_m].reshape(all_rows, HEAD_DIM).astype(f32)

    def spread(rows8):
        return jnp.concatenate(
            [jnp.broadcast_to(rows8[kv : kv + 1], (block_rows, HEAD_DIM)) for kv in range(KV_HEADS)], axis=0
        )

    second = lax.broadcasted_iota(jnp.int32, (all_rows, 1), 0) % block_rows >= group
    first_score = jnp.sum(query_all * spread(row_keys[me_m, 0]), axis=-1, keepdims=True) * score_scale
    next_score = jnp.sum(query_all * spread(row_keys[me_m, 1]), axis=-1, keepdims=True) * score_scale
    top = jnp.maximum(first_score, jnp.where(second, next_score, -1e30))
    for d in range(1, mdl_count):
        stat_copy(d).wait()
        part_copy(d).wait()
    held = [stats[0]] + [recv_stats[d] for d in range(1, mdl_count)]
    part_tops = [to_col(s[0, :1]) for s in held]
    part_sums = [to_col(s[1, :1]) for s in held]
    for part_top in part_tops:
        top = jnp.maximum(top, part_top)
    first_weight = jnp.exp(first_score - top)
    next_weight = jnp.where(second, jnp.exp(jnp.where(second, next_score, -1e30) - top), 0.0)
    total = first_weight + next_weight
    combined = first_weight.astype(bf16).astype(f32) * spread(row_values[me_m, 0]) + next_weight.astype(bf16).astype(
        f32
    ) * spread(row_values[me_m, 1])
    for d in range(mdl_count):
        factor = jnp.exp(part_tops[d] - top)
        acc = send3[0] if d == 0 else recv3[d]
        total = total + part_sums[d] * factor
        combined = combined + acc.reshape(all_rows, HEAD_DIM).astype(f32) * factor
    attended = (combined / total).astype(bf16)
    send4[...] = attended.reshape(send4.shape)
    recv4[me_h, me_m] = send4[me_h]
    copies = []
    for k, (dh, dm) in enumerate(others):
        to = partner(dh, dm)
        copy = send(send4.at[to["hid"]], recv4.at[me_h, me_m], s4.at[k], r4.at[k], to)
        copy.start()
        copies.append(copy)
    for copy in copies:
        copy.wait()
    heads_f32[...] = recv4[...].astype(f32).reshape(heads_f32.shape)
    senders = hid_count * mdl_count
    for j in range(query_heads):
        kv, g = j // group, j % group
        both = [
            heads_f32[pl.ds(kv * block_rows + t * group + g, senders, stride=pair_rows), :] for t in range(2)
        ]
        heads_in[:, j * HEAD_DIM : (j + 1) * HEAD_DIM] = jnp.concatenate(both, axis=0).astype(bf16)
    out_load.wait()
    partial_out[...] = jnp.dot(heads_in[...], out_w[...], preferred_element_type=f32)
    for h in range(hid_count):
        low = h * mdl_count
        send5[h] = jnp.concatenate(
            [partial_out[low : low + mdl_count], partial_out[senders + low : senders + low + mdl_count]], axis=0
        ).astype(bf16)
    copies = []
    for d in range(1, hid_count):
        to = lax.rem(me_h + d, hid_count)
        copy = send(send5.at[to], recv5.at[d], s5.at[d], r5.at[d], {"hid": to})
        copy.start()
        copies.append(copy)
    for copy in copies:
        copy.wait()
    summed = send5[me_h].astype(f32)
    for d in range(1, hid_count):
        summed = summed + recv5[d].astype(f32)
    result_ref[...] = summed.astype(bf16)


def fused_body(
    tokens,
    norm_gain,
    query_weight,
    key_weight,
    value_weight,
    query_bias,
    key_bias,
    value_bias,
    out_weight,
    key_cache,
    value_cache,
    lengths,
):
    row_count, steps_count, width = tokens.shape
    hid_count, mdl_count = lax.axis_size("hid"), lax.axis_size("mdl")
    local_rows, local_len = key_cache.shape[:2]
    rows = row_count * steps_count
    own_rows = rows // hid_count
    proj_width = query_weight.shape[1] + 2 * key_weight.shape[1]
    block_width = proj_width // mdl_count
    heads_out = block_width // HEAD_DIM
    group = HEADS // KV_HEADS
    block_rows = steps_count * group
    kv_local = KV_HEADS // hid_count
    out_width = out_weight.shape[1]
    others = hid_count * mdl_count - 1
    bias = jnp.concatenate([query_bias, key_bias, value_bias]).astype(jnp.float32)
    bias = bias.reshape(mdl_count, heads_out, 1, HEAD_DIM)
    half = HEAD_DIM // 2
    freq = jnp.asarray((rope_base ** (-2.0 * (np.arange(HEAD_DIM) % half) / HEAD_DIM)).astype(np.float32)[None])
    bf16, f32 = jnp.bfloat16, jnp.float32
    vmem, hbm = pl.BlockSpec(memory_space=pltpu.VMEM), pl.BlockSpec(memory_space=pl.ANY)
    dma = pltpu.SemaphoreType.DMA
    result = pl.pallas_call(
        fused_kernel,
        out_shape=jax.ShapeDtypeStruct((own_rows, out_width), bf16),
        in_specs=[vmem, vmem, vmem, vmem, pl.BlockSpec(memory_space=pltpu.SMEM)] + [hbm] * 6,
        out_specs=vmem,
        scratch_shapes=[
            pltpu.VMEM((mdl_count, width, block_width), bf16),
            pltpu.VMEM(out_weight.shape, bf16),
            pltpu.VMEM(key_cache.shape, bf16),
            pltpu.VMEM(value_cache.shape, bf16),
            pltpu.VMEM((mdl_count, heads_out, rows, HEAD_DIM), bf16),
            pltpu.VMEM((mdl_count, heads_out, rows, HEAD_DIM), bf16),
            pltpu.VMEM((8, 128), f32),
            pltpu.VMEM((mdl_count, 8, 128), f32),
            pltpu.VMEM((hid_count, heads_out, own_rows, HEAD_DIM), bf16),
            pltpu.VMEM((hid_count, mdl_count, heads_out, own_rows, HEAD_DIM), bf16),
            pltpu.VMEM((HEADS * own_rows, HEAD_DIM), f32),
            pltpu.VMEM((KV_HEADS * own_rows, HEAD_DIM), f32),
            pltpu.VMEM((KV_HEADS * own_rows, HEAD_DIM), f32),
            pltpu.VMEM((local_rows, KV_HEADS, block_rows, HEAD_DIM), bf16),
            pltpu.VMEM((local_rows, steps_count, KV_HEADS, HEAD_DIM), f32),
            pltpu.VMEM((local_rows, steps_count, KV_HEADS, HEAD_DIM), f32),
            pltpu.VMEM((mdl_count, KV_HEADS, block_rows, HEAD_DIM), bf16),
            pltpu.VMEM((mdl_count, KV_HEADS, block_rows, HEAD_DIM), bf16),
            pltpu.VMEM((mdl_count, 2, 8, 128), f32),
            pltpu.VMEM((mdl_count, 2, 8, 128), f32),
            pltpu.VMEM((hid_count, kv_local * block_rows, HEAD_DIM), bf16),
            pltpu.VMEM((hid_count, mdl_count, kv_local * block_rows, HEAD_DIM), bf16),
            pltpu.VMEM((hid_count * mdl_count * kv_local * block_rows, HEAD_DIM), f32),
            pltpu.VMEM((rows, out_weight.shape[0]), bf16),
            pltpu.VMEM((rows, out_width), f32),
            pltpu.VMEM((hid_count, own_rows, out_width), bf16),
            pltpu.VMEM((hid_count, own_rows, out_width), bf16),
            dma((mdl_count + 5,)),
            dma((mdl_count,)), dma((mdl_count,)),
            dma((mdl_count,)), dma((mdl_count,)),
            dma((others,)), dma((others,)),
            dma((mdl_count,)), dma((mdl_count,)),
            dma((mdl_count,)), dma((mdl_count,)),
            dma((others,)), dma((others,)),
            dma((hid_count,)), dma((hid_count,)),
        ],
        compiler_params=pltpu.CompilerParams(
            collective_id=0, has_side_effects=True, vmem_limit_bytes=52 * 2**20
        ),
    )(
        tokens.reshape(rows, width), norm_gain.reshape(1, width), bias, freq, lengths,
        query_weight, key_weight, value_weight, out_weight, key_cache, value_cache,
    )
    return result.reshape(steps_count, local_rows, out_width).transpose(1, 0, 2)


def choose(*arrays):
    tokens, query_weight, key_weight, key_cache = arrays[0], arrays[2], arrays[3], arrays[9]
    hid_count, mdl_count = lax.axis_size("hid"), lax.axis_size("mdl")
    proj_width = query_weight.shape[1] + 2 * key_weight.shape[1]
    fits = (
        tokens.shape[1] == 2
        and key_cache.shape[0] == mdl_count
        and key_weight.shape[1] == 2 * HEAD_DIM
        and KV_HEADS == 2 * hid_count
        and proj_width % (mdl_count * HEAD_DIM) == 0
        and tokens.shape[0] * 2 <= 128
    )
    return (fused_body if fits else body)(*arrays)


def solution(mesh):
    placed = (
        P("groups", None, "mdl"),
        P("mdl"),
        P("mdl", "hid"),
        P("mdl", "hid"),
        P("mdl", "hid"),
        P("hid"),
        P("hid"),
        P("hid"),
        P("hid", "mdl"),
        P(("groups", "hid"), "mdl", None),
        P(("groups", "hid"), "mdl", None),
        P("groups"),
    )
    return jax.shard_map(
        choose,
        mesh=mesh,
        in_specs=placed,
        out_specs=P(("groups", "hid"), None, "mdl"),
        check_vma=False,
    )
```

```python
import math

import jax
import jax.numpy as jnp
import numpy as np
from jax import lax
from jax.experimental import pallas as pl
from jax.experimental.pallas import tpu as pltpu
from jax.sharding import PartitionSpec as P

D = 8192
HEADS = 64
KV_HEADS = 8
HEAD_DIM = 128


epsilon = 1e-06
rope_base = 1000000.0


def combined_all(value, axis, combine):
    everything = jax.tree.map(
        lambda part, kind: lax.all_gather(part.astype(kind), axis),
        value,
        (jnp.bfloat16, jnp.bfloat16, jnp.bfloat16),
    )

    def take(k):
        return jax.tree.map(lambda part, own: part[k].astype(own.dtype), everything, value)

    return lax.fori_loop(
        1, lax.axis_size(axis), lambda k, so_far: combine(so_far, take(k)), take(0)
    )


def rotate_pairs(values, positions):
    half = values.shape[-1] // 2
    freq = rope_base ** (-jnp.arange(half, dtype=jnp.float32) * 2.0 / values.shape[-1])
    angles = positions.astype(jnp.float32)[..., None, None] * freq
    cosine = jnp.cos(angles)
    sine = jnp.sin(angles)
    lower = values[..., :half]
    upper = values[..., half:]
    return jnp.concatenate([lower * cosine - upper * sine, upper * cosine + lower * sine], axis=-1)


def join_parts(left_part, right_part):
    left_max, left_sum, left_acc = left_part
    right_max, right_sum, right_acc = right_part
    joined_max = jnp.maximum(left_max, right_max)
    left_factor = jnp.exp(left_max - joined_max)
    right_factor = jnp.exp(right_max - joined_max)
    joined_sum = left_sum * left_factor + right_sum * right_factor
    joined_acc = left_acc * left_factor[..., None] + right_acc * right_factor[..., None]
    return (joined_max, joined_sum, joined_acc)


def body(
    tokens,
    norm_gain,
    query_weight,
    key_weight,
    value_weight,
    query_bias,
    key_bias,
    value_bias,
    out_weight,
    key_cache,
    value_cache,
    lengths,
):
    row_count = tokens.shape[0]
    steps_count = tokens.shape[1]
    hid_count = lax.axis_size("hid")
    local_rows = key_cache.shape[0]
    local_len = key_cache.shape[1]
    group = HEADS // KV_HEADS
    query_width = query_weight.shape[1]
    key_width = key_weight.shape[1]
    proj_width = query_width + 2 * key_width
    inputs = tokens.astype(jnp.float32)
    square_sum = lax.psum(jnp.sum(inputs * inputs, axis=-1), "mdl")
    inv_rms = lax.rsqrt(square_sum / D + epsilon)
    row_scale = inv_rms.reshape(row_count * steps_count, 1)
    scaled = (
        (inputs * norm_gain.astype(jnp.float32))
        .astype(jnp.bfloat16)
        .reshape(row_count * steps_count, -1)
    )
    partial_value = jnp.concatenate(
        [
            jnp.dot(scaled, query_weight, preferred_element_type=jnp.float32),
            jnp.dot(scaled, key_weight, preferred_element_type=jnp.float32),
            jnp.dot(scaled, value_weight, preferred_element_type=jnp.float32),
        ],
        axis=1,
    )
    all_bias = jnp.concatenate([query_bias, key_bias, value_bias]).astype(jnp.float32)
    summed = lax.psum(partial_value.astype(jnp.bfloat16), "mdl").astype(jnp.float32)
    projected = (
        (summed * row_scale + all_bias)
        .astype(jnp.bfloat16)
        .reshape(row_count, steps_count, proj_width)
    )
    arrived = lax.all_to_all(projected, "hid", split_axis=0, concat_axis=2, tiled=True)
    blocks = arrived.reshape(local_rows, steps_count, hid_count, proj_width)
    query_lin = blocks[..., :query_width].reshape(local_rows, steps_count, HEADS, HEAD_DIM)
    key_lin = blocks[..., query_width : query_width + key_width].reshape(
        local_rows, steps_count, KV_HEADS, HEAD_DIM
    )
    value_new = blocks[..., query_width + key_width :].reshape(
        local_rows, steps_count, KV_HEADS, HEAD_DIM
    )
    my_lengths = lax.dynamic_slice_in_dim(
        lengths, lax.axis_index("hid") * local_rows, local_rows, 0
    )
    positions = my_lengths[:, None] + jnp.arange(steps_count, dtype=jnp.int32)[None, :]
    queries = rotate_pairs(query_lin.astype(jnp.float32), positions).astype(jnp.bfloat16)
    key_new = rotate_pairs(key_lin.astype(jnp.float32), positions).astype(jnp.bfloat16)
    grouped = queries.reshape(local_rows, steps_count, KV_HEADS, group, HEAD_DIM).transpose(
        0, 2, 1, 3, 4
    )
    grouped = grouped.reshape(local_rows, KV_HEADS, steps_count * group, HEAD_DIM)
    cache_keys = key_cache.reshape(local_rows, local_len, KV_HEADS, HEAD_DIM)
    cache_values = value_cache.reshape(local_rows, local_len, KV_HEADS, HEAD_DIM)
    score_scale = 1.0 / math.sqrt(HEAD_DIM)
    scores = (
        jnp.einsum("rkqd,rskd->rkqs", grouped, cache_keys, preferred_element_type=jnp.float32)
        * score_scale
    )
    cache_place = lax.axis_index("mdl") * local_len + jnp.arange(local_len, dtype=jnp.int32)
    visible = (cache_place[None, :] < my_lengths[:, None])[:, None, None, :]
    masked = jnp.where(visible, scores, -1e30)
    local_max = jnp.max(masked, axis=-1)
    weights = jnp.where(visible, jnp.exp(masked - local_max[..., None]), 0.0)
    local_sum = jnp.sum(weights, axis=-1)
    local_acc = jnp.einsum(
        "rkqs,rskd->rkqd",
        weights.astype(jnp.bfloat16),
        cache_values,
        preferred_element_type=jnp.float32,
    )
    run_max, run_sum, run_acc = combined_all((local_max, local_sum, local_acc), "mdl", join_parts)
    new_scores = (
        jnp.einsum("rkqd,rukd->rkqu", grouped, key_new, preferred_element_type=jnp.float32)
        * score_scale
    )
    query_step = jnp.arange(steps_count * group, dtype=jnp.int32) // group
    causal = (jnp.arange(steps_count, dtype=jnp.int32)[None, :] <= query_step[:, None])[None, None]
    new_masked = jnp.where(causal, new_scores, -1e30)
    new_max = jnp.maximum(run_max, jnp.max(new_masked, axis=-1))
    shrink = jnp.exp(run_max - new_max)
    new_weights = jnp.where(causal, jnp.exp(new_masked - new_max[..., None]), 0.0)
    total = run_sum * shrink + jnp.sum(new_weights, axis=-1)
    combined = run_acc * shrink[..., None] + jnp.einsum(
        "rkqu,rukd->rkqd",
        new_weights.astype(jnp.bfloat16),
        value_new,
        preferred_element_type=jnp.float32,
    )
    attended = combined / total[..., None]
    attended = attended.reshape(local_rows, KV_HEADS, steps_count, group, HEAD_DIM).transpose(
        0, 2, 1, 3, 4
    )
    attended = attended.reshape(local_rows, steps_count, HEADS * HEAD_DIM).astype(jnp.bfloat16)
    by_heads = lax.all_to_all(attended, "hid", split_axis=2, concat_axis=0, tiled=True)
    flat_heads = by_heads.reshape(row_count * steps_count, query_width)
    result = lax.psum_scatter(
        jnp.dot(flat_heads, out_weight, preferred_element_type=jnp.float32).astype(jnp.bfloat16),
        "hid",
        scatter_dimension=0,
        tiled=True,
    )
    return result.reshape(local_rows, steps_count, -1)

def fused_kernel(
    tokens_hbm, gain_hbm, query_bias_hbm, key_bias_hbm, value_bias_hbm, freq_hbm, lengths_ref,
    query_hbm, key_hbm, value_hbm, out_hbm, keys_hbm, values_hbm,
    result_ref,
    tokens_in, gain_in, query_bias, key_bias, value_bias, freq_in, bias,
    proj_w, out_w, keys, values,
    send1, recv1, squares, recv_squares, send2, recv2, rotated, key_rot, value_rot, row_queries,
    send3, recv3, stats, recv_stats, send4, recv4, heads_f32, heads_in, send5, recv5,
    load_sem, block_sem, s1, r1, sq_s, sq_r, s2, r2, s3, r3, st_s, st_r, s4, r4, s5, r5,
):
    hid_count, mdl_count = lax.axis_size("hid"), lax.axis_size("mdl")
    me_h, me_m = lax.axis_index("hid"), lax.axis_index("mdl")
    bf16, f32 = jnp.bfloat16, jnp.float32
    rows = tokens_in.shape[0] * tokens_in.shape[1]
    own_rows = rows // hid_count
    local_rows, local_len = keys.shape[0], keys.shape[1]
    block_width = proj_w.shape[2]
    heads_out = block_width // HEAD_DIM
    query_width, key_width = query_hbm.shape[1], key_hbm.shape[1]
    query_heads = query_width // HEAD_DIM
    kv_local = key_width // HEAD_DIM
    group = HEADS // KV_HEADS
    block_rows = 2 * group
    pair_rows = 2 * block_rows
    far_first = (2, 3, 1, 0)

    def other(me, d):
        if d == 0:
            return me
        if d == 1:
            return me + 1 - 2 * lax.rem(me, 2)
        if d == 2:
            return lax.rem(me + 2, 4)
        return 3 - me

    def send(src, dst, send_sem, recv_sem, to):
        return pltpu.make_async_remote_copy(
            src_ref=src, dst_ref=dst, send_sem=send_sem, recv_sem=recv_sem,
            device_id=to, device_id_type=pl.DeviceIdType.MESH,
        )

    def partner(dh, dm):
        return {"hid": other(me_h, dh), "mdl": other(me_m, dm)}

    others = [(dh, dm) for dh in range(hid_count) for dm in far_first if dh or dm]
    barrier = pltpu.get_barrier_semaphore()
    for dh, dm in others:
        pl.semaphore_signal(barrier, inc=1, device_id=partner(dh, dm), device_id_type=pl.DeviceIdType.MESH)

    loads = []

    def load(src, dst):
        copy = pltpu.make_async_copy(src, dst, load_sem.at[len(loads)])
        copy.start()
        loads.append(copy)
        return copy

    small = [
        load(tokens_hbm, tokens_in), load(gain_hbm, gain_in), load(query_bias_hbm, query_bias),
        load(key_bias_hbm, key_bias), load(value_bias_hbm, value_bias), load(freq_hbm, freq_in),
    ]
    last = mdl_count - 1
    tail = query_width - last * block_width
    for d in far_first:
        b = other(me_m, d)

        @pl.when(b < last)
        def _(b=b):
            columns = pl.ds(pl.multiple_of(b * block_width, 128), block_width)
            pltpu.make_async_copy(query_hbm.at[:, columns], proj_w.at[b], block_sem.at[b]).start()

        @pl.when(b == last)
        def _():
            dst, sem = proj_w.at[last], block_sem.at[last]
            pltpu.make_async_copy(query_hbm.at[:, last * block_width : query_width], dst.at[:, :tail], sem).start()
            pltpu.make_async_copy(key_hbm, dst.at[:, tail : tail + key_width], sem).start()
            pltpu.make_async_copy(value_hbm, dst.at[:, tail + key_width : block_width], sem).start()

    keys_load = load(keys_hbm, keys)
    values_load = load(values_hbm, values)
    out_load = load(out_hbm, out_w)
    for copy in small:
        copy.wait()

    inputs = tokens_in[...].astype(f32).reshape(rows, -1)
    square_col = jnp.sum(inputs * inputs, axis=-1, keepdims=True)
    eye_row = lax.broadcasted_iota(jnp.int32, (rows, 128), 0)
    eye_lane = lax.broadcasted_iota(jnp.int32, (rows, 128), 1)
    eye_in = eye_row == eye_lane
    square_row = jnp.sum(jnp.where(eye_in, square_col, 0.0), axis=0, keepdims=True)
    squares[...] = jnp.broadcast_to(square_row, squares.shape)
    scaled = (inputs * gain_in[...].astype(f32).reshape(1, -1)).astype(bf16)
    all_bias = jnp.concatenate(
        [ref[...].astype(f32).reshape(1, -1) for ref in (query_bias, key_bias, value_bias)], axis=1
    )
    for b in range(mdl_count):
        bias[b] = all_bias[:, b * block_width : (b + 1) * block_width]
    pl.semaphore_wait(barrier, len(others))

    sends = []
    square_copies, block_copies = {}, {}
    for d in far_first[:-1]:
        square_copies[d] = send(squares, recv_squares.at[d], sq_s.at[d], sq_r.at[d], partner(0, d))
        square_copies[d].start()
    for d in far_first:
        b = other(me_m, d)
        pltpu.make_async_copy(proj_w.at[b], proj_w.at[b], block_sem.at[b]).wait()
        part = jnp.dot(scaled, proj_w[b], preferred_element_type=f32).astype(bf16)
        for i in range(heads_out):
            send1[b, i] = part[:, i * HEAD_DIM : (i + 1) * HEAD_DIM]
        if d:
            block_copies[d] = send(send1.at[b], recv1.at[d], s1.at[d], r1.at[d], partner(0, d))
            block_copies[d].start()

    place = lax.broadcasted_iota(jnp.int32, (own_rows, HEAD_DIM), 0)
    lane = lax.broadcasted_iota(jnp.int32, (own_rows, HEAD_DIM), 1)
    position = place % 2
    for r in range(local_rows):
        position = position + jnp.where(place // 2 == r, lengths_ref[me_h * local_rows + r], 0)
    half = HEAD_DIM // 2
    angles = position.astype(f32) * freq_in[...]
    cosine = jnp.cos(angles)
    sine = jnp.sin(angles)
    sine = jnp.where(lane < half, -sine, sine)

    square_total = squares[...]
    for d, copy in square_copies.items():
        copy.wait()
        square_total = square_total + recv_squares[d]
    square_sum = jnp.sum(jnp.where(eye_in, square_total[:1, :], 0.0), axis=1, keepdims=True)
    inv_rms = lax.rsqrt(square_sum / D + epsilon)
    my_bias = bias[me_m]
    for copy in block_copies.values():
        copy.wait()
    for i in range(heads_out):
        total = send1[me_m, i].astype(f32)
        for d in block_copies:
            total = total + recv1[d, i].astype(f32)
        total = total * inv_rms + my_bias[:, i * HEAD_DIM : (i + 1) * HEAD_DIM]
        for h in range(hid_count):
            send2[h, i] = total[h * own_rows : (h + 1) * own_rows].astype(bf16)
    row_copies = {}
    for dh, dm in others:
        k = dh * mdl_count + dm
        row_copies[dh, dm] = send(
            send2.at[other(me_h, dh)], recv2.at[me_h, me_m], s2.at[k], r2.at[k], partner(dh, dm)
        )
        row_copies[dh, dm].start()
    sends += row_copies.values()
    recv2[me_h, me_m] = send2[me_h]

    score_scale = 1.0 / math.sqrt(HEAD_DIM)
    columns = lax.broadcasted_iota(jnp.int32, (pair_rows, local_len), 1)
    pair_row = lax.broadcasted_iota(jnp.int32, (pair_rows, 128), 0)
    pair_lane = lax.broadcasted_iota(jnp.int32, (pair_rows, 128), 1)
    top_place = pair_row == pair_lane
    sum_place = pair_row + pair_rows == pair_lane
    part_copies, stat_copies, head_copies = {}, {}, {}

    def prepare(dh):
        h = other(me_h, dh)
        for dm in far_first:
            if dh or dm:
                row_copies[dh, dm].wait_recv()
        x = recv2[h].astype(f32).reshape(mdl_count * heads_out, own_rows, HEAD_DIM)
        turned_heads = query_heads + kv_local
        turn = x[:turned_heads]
        swapped = pltpu.roll(turn.reshape(turned_heads * own_rows, HEAD_DIM), half, 1)
        turned = turn * cosine[None] + swapped.reshape(turned_heads, own_rows, HEAD_DIM) * sine[None]
        n = query_heads * own_rows
        rotated[dh * n : (dh + 1) * n] = turned[:query_heads].reshape(n, HEAD_DIM)
        k = kv_local * own_rows
        key_rot[dh * k : (dh + 1) * k] = turned[query_heads:].astype(bf16).astype(f32).reshape(k, HEAD_DIM)
        value_rot[dh * k : (dh + 1) * k] = x[turned_heads:].reshape(k, HEAD_DIM)
        for r in range(local_rows):
            steps = [rotated[pl.ds(dh * n + 2 * r + t, query_heads, stride=own_rows), :] for t in range(2)]
            for kv in range(kv_local):
                row_queries[r, dh * kv_local + kv] = jnp.concatenate(
                    [step[kv * group : (kv + 1) * group] for step in steps], axis=0
                ).astype(bf16)

    def attend(dh):
        wide = pl.ds(pl.multiple_of(other(me_h, dh) * 2 * HEAD_DIM, 2 * HEAD_DIM), 2 * HEAD_DIM)
        for d in far_first:
            r = other(me_m, d)
            visible = columns < lengths_ref[me_h * local_rows + r] - me_m * local_len
            qa, qb = row_queries[r, 2 * dh], row_queries[r, 2 * dh + 1]
            none = jnp.zeros_like(qa)
            left = jnp.concatenate(
                [jnp.concatenate([qa, none], axis=1), jnp.concatenate([none, qb], axis=1)], axis=0
            )
            scores = lax.dot_general(
                left, keys[r, :, wide], (((1,), (1,)), ((), ())), preferred_element_type=f32
            ) * score_scale
            masked = jnp.where(visible, scores, -1e30)
            top = jnp.max(masked, axis=-1, keepdims=True)
            weights = jnp.where(visible, jnp.exp(masked - top), 0.0)
            total = jnp.sum(weights, axis=-1, keepdims=True)
            acc = jnp.dot(weights.astype(bf16), values[r, :, wide], preferred_element_type=f32)
            send3[dh, d, 0] = acc[:block_rows, :HEAD_DIM].astype(bf16)
            send3[dh, d, 1] = acc[block_rows:, HEAD_DIM:].astype(bf16)
            packed = jnp.where(top_place, top, 0.0) + jnp.where(sum_place, total, 0.0)
            stats[dh, d] = jnp.broadcast_to(jnp.sum(packed, axis=0, keepdims=True), (8, 128))
            if d:
                k = dh * mdl_count + d
                to = partner(0, d)
                part_copies[dh, d] = send(send3.at[dh, d], recv3.at[dh, d], s3.at[k], r3.at[k], to)
                stat_copies[dh, d] = send(stats.at[dh, d], recv_stats.at[dh, d], st_s.at[k], st_r.at[k], to)
                part_copies[dh, d].start()
                stat_copies[dh, d].start()
                sends.append(part_copies[dh, d])
                sends.append(stat_copies[dh, d])

    second = lax.broadcasted_iota(jnp.int32, (pair_rows, 1), 0) % block_rows >= group

    def new_part(ref, dh, t):
        both = ref[pl.ds(dh * kv_local * own_rows + 2 * me_m + t, kv_local, stride=own_rows), :]
        return jnp.concatenate(
            [jnp.broadcast_to(both[kv : kv + 1], (block_rows, HEAD_DIM)) for kv in range(kv_local)], axis=0
        )

    def combine(dh):
        query = jnp.concatenate([row_queries[me_m, 2 * dh], row_queries[me_m, 2 * dh + 1]], axis=0).astype(f32)
        first_score = jnp.sum(query * new_part(key_rot, dh, 0), axis=-1, keepdims=True) * score_scale
        next_score = jnp.sum(query * new_part(key_rot, dh, 1), axis=-1, keepdims=True) * score_scale
        next_score = jnp.where(second, next_score, -1e30)
        top = jnp.maximum(first_score, next_score)
        for d in far_first[:-1]:
            stat_copies[dh, d].wait_recv()
            part_copies[dh, d].wait_recv()
        held = [stats[dh, 0] if d == 0 else recv_stats[dh, d] for d in far_first]
        tops = [jnp.sum(jnp.where(top_place, x[:1], 0.0), axis=1, keepdims=True) for x in held]
        sums = [jnp.sum(jnp.where(sum_place, x[:1], 0.0), axis=1, keepdims=True) for x in held]
        for part_top in tops:
            top = jnp.maximum(top, part_top)
        first_weight = jnp.exp(first_score - top)
        next_weight = jnp.where(second, jnp.exp(next_score - top), 0.0)
        total = first_weight + next_weight
        mixed = first_weight.astype(bf16).astype(f32) * new_part(value_rot, dh, 0)
        mixed = mixed + next_weight.astype(bf16).astype(f32) * new_part(value_rot, dh, 1)
        for n, d in enumerate(far_first):
            factor = jnp.exp(tops[n] - top)
            acc = send3[dh, 0] if d == 0 else recv3[dh, d]
            total = total + sums[n] * factor
            mixed = mixed + acc.reshape(pair_rows, HEAD_DIM).astype(f32) * factor
        send4[dh] = (mixed / total).astype(bf16)
        for dm in far_first:
            if dh or dm:
                k = dh * mdl_count + dm
                head_copies[dh, dm] = send(
                    send4.at[dh], recv4.at[me_h, me_m], s4.at[k], r4.at[k], partner(dh, dm)
                )
                head_copies[dh, dm].start()
                sends.append(head_copies[dh, dm])
            else:
                recv4[me_h, me_m] = send4[0]

    prepare(0)
    keys_load.wait()
    values_load.wait()
    for dh in range(hid_count):
        attend(dh)
        if dh + 1 < hid_count:
            prepare(dh + 1)
        if dh:
            combine(dh - 1)
    combine(hid_count - 1)

    for copy in head_copies.values():
        copy.wait_recv()
    heads_f32[...] = recv4[...].astype(f32).reshape(heads_f32.shape)
    senders = hid_count * mdl_count
    for j in range(query_heads):
        kv, g = j // group, j % group
        both = [
            heads_f32[pl.ds(kv * block_rows + t * group + g, senders, stride=pair_rows), :] for t in range(2)
        ]
        heads_in[:, j * HEAD_DIM : (j + 1) * HEAD_DIM] = jnp.concatenate(both, axis=0).astype(bf16)
    out_load.wait()
    chunks, chunk_width = send5.shape[1], send5.shape[3]
    out_copies = {}
    for c in range(chunks):
        part = jnp.dot(
            heads_in[...], out_w[:, c * chunk_width : (c + 1) * chunk_width], preferred_element_type=f32
        )
        for h in range(hid_count):
            low = h * mdl_count
            send5[h, c] = jnp.concatenate(
                [part[low : low + mdl_count], part[senders + low : senders + low + mdl_count]], axis=0
            ).astype(bf16)
        for d in far_first[:-1]:
            k = d * chunks + c
            out_copies[d, c] = send(
                send5.at[other(me_h, d), c], recv5.at[d, c], s5.at[k], r5.at[k], partner(d, 0)
            )
            out_copies[d, c].start()
    sends += out_copies.values()
    for c in range(chunks):
        summed = send5[me_h, c].astype(f32)
        for d in far_first[:-1]:
            out_copies[d, c].wait_recv()
            summed = summed + recv5[d, c].astype(f32)
        result_ref[:, c * chunk_width : (c + 1) * chunk_width] = summed.astype(bf16)
    for copy in sends:
        copy.wait_send()


def fused_body(
    tokens,
    norm_gain,
    query_weight,
    key_weight,
    value_weight,
    query_bias,
    key_bias,
    value_bias,
    out_weight,
    key_cache,
    value_cache,
    lengths,
):
    row_count, steps_count, width = tokens.shape
    hid_count, mdl_count = lax.axis_size("hid"), lax.axis_size("mdl")
    local_rows, local_len = key_cache.shape[:2]
    rows = row_count * steps_count
    own_rows = rows // hid_count
    proj_width = query_weight.shape[1] + 2 * key_weight.shape[1]
    block_width = proj_width // mdl_count
    heads_out = block_width // HEAD_DIM
    group = HEADS // KV_HEADS
    block_rows = steps_count * group
    kv_local = KV_HEADS // hid_count
    out_width = out_weight.shape[1]
    pairs = hid_count * mdl_count
    chunks = 2
    half = HEAD_DIM // 2
    freq = jnp.asarray((rope_base ** (-2.0 * (np.arange(HEAD_DIM) % half) / HEAD_DIM)).astype(np.float32)[None])
    bf16, f32 = jnp.bfloat16, jnp.float32
    vmem, hbm = pl.BlockSpec(memory_space=pltpu.VMEM), pl.BlockSpec(memory_space=pl.ANY)
    dma = pltpu.SemaphoreType.DMA
    result = pl.pallas_call(
        fused_kernel,
        out_shape=jax.ShapeDtypeStruct((own_rows, out_width), bf16),
        in_specs=[hbm] * 6 + [pl.BlockSpec(memory_space=pltpu.SMEM)] + [hbm] * 6,
        out_specs=vmem,
        scratch_shapes=[
            pltpu.VMEM(tokens.shape, bf16),
            pltpu.VMEM(norm_gain.shape, bf16),
            pltpu.VMEM(query_bias.shape, bf16),
            pltpu.VMEM(key_bias.shape, bf16),
            pltpu.VMEM(value_bias.shape, bf16),
            pltpu.VMEM((1, HEAD_DIM), f32),
            pltpu.VMEM((mdl_count, 1, block_width), f32),
            pltpu.VMEM((mdl_count, width, block_width), bf16),
            pltpu.VMEM(out_weight.shape, bf16),
            pltpu.VMEM(key_cache.shape, bf16),
            pltpu.VMEM(value_cache.shape, bf16),
            pltpu.VMEM((mdl_count, heads_out, rows, HEAD_DIM), bf16),
            pltpu.VMEM((mdl_count, heads_out, rows, HEAD_DIM), bf16),
            pltpu.VMEM((8, 128), f32),
            pltpu.VMEM((mdl_count, 8, 128), f32),
            pltpu.VMEM((hid_count, heads_out, own_rows, HEAD_DIM), bf16),
            pltpu.VMEM((hid_count, mdl_count, heads_out, own_rows, HEAD_DIM), bf16),
            pltpu.VMEM((HEADS * own_rows, HEAD_DIM), f32),
            pltpu.VMEM((KV_HEADS * own_rows, HEAD_DIM), f32),
            pltpu.VMEM((KV_HEADS * own_rows, HEAD_DIM), f32),
            pltpu.VMEM((local_rows, KV_HEADS, block_rows, HEAD_DIM), bf16),
            pltpu.VMEM((hid_count, mdl_count, kv_local, block_rows, HEAD_DIM), bf16),
            pltpu.VMEM((hid_count, mdl_count, kv_local, block_rows, HEAD_DIM), bf16),
            pltpu.VMEM((hid_count, mdl_count, 8, 128), f32),
            pltpu.VMEM((hid_count, mdl_count, 8, 128), f32),
            pltpu.VMEM((hid_count, kv_local * block_rows, HEAD_DIM), bf16),
            pltpu.VMEM((hid_count, mdl_count, kv_local * block_rows, HEAD_DIM), bf16),
            pltpu.VMEM((pairs * kv_local * block_rows, HEAD_DIM), f32),
            pltpu.VMEM((rows, out_weight.shape[0]), bf16),
            pltpu.VMEM((hid_count, chunks, own_rows, out_width // chunks), bf16),
            pltpu.VMEM((hid_count, chunks, own_rows, out_width // chunks), bf16),
            dma((9,)), dma((mdl_count,)),
            dma((mdl_count,)), dma((mdl_count,)),
            dma((mdl_count,)), dma((mdl_count,)),
            dma((pairs,)), dma((pairs,)),
            dma((pairs,)), dma((pairs,)),
            dma((pairs,)), dma((pairs,)),
            dma((pairs,)), dma((pairs,)),
            dma((hid_count * chunks,)), dma((hid_count * chunks,)),
        ],
        compiler_params=pltpu.CompilerParams(
            collective_id=0, has_side_effects=True, vmem_limit_bytes=60 * 2**20
        ),
    )(
        tokens, norm_gain, query_bias, key_bias, value_bias, freq, lengths,
        query_weight, key_weight, value_weight, out_weight, key_cache, value_cache,
    )
    return result.reshape(steps_count, local_rows, out_width).transpose(1, 0, 2)


def choose(*arrays):
    tokens, query_weight, key_weight, key_cache = arrays[0], arrays[2], arrays[3], arrays[9]
    hid_count, mdl_count = lax.axis_size("hid"), lax.axis_size("mdl")
    proj_width = query_weight.shape[1] + 2 * key_weight.shape[1]
    fits = (
        tokens.shape[1] == 2
        and mdl_count == 4
        and key_cache.shape[0] == mdl_count
        and key_weight.shape[1] == 2 * HEAD_DIM
        and KV_HEADS == 2 * hid_count
        and proj_width % (mdl_count * HEAD_DIM) == 0
        and (mdl_count - 1) * proj_width <= mdl_count * query_weight.shape[1]
        and tokens.shape[0] * 2 <= 128
    )
    return (fused_body if fits else body)(*arrays)


def solution(mesh):
    placed = (
        P("groups", None, "mdl"),
        P("mdl"),
        P("mdl", "hid"),
        P("mdl", "hid"),
        P("mdl", "hid"),
        P("hid"),
        P("hid"),
        P("hid"),
        P("hid", "mdl"),
        P(("groups", "hid"), "mdl", None),
        P(("groups", "hid"), "mdl", None),
        P("groups"),
    )
    return jax.shard_map(
        choose,
        mesh=mesh,
        in_specs=placed,
        out_specs=P(("groups", "hid"), None, "mdl"),
        check_vma=False,
    )
```
